256 devices in a mesh: queue: 16 (over y, z_lo), seq: 16 (over z_hi, x, core).
Axes of the slice: x: 4, y: 4, z: 8 (z_hi: 2, z_lo: 4; z = z_hi * 4 + z_lo), core: 2. Of those that a mesh axis runs over, the one named last changes fastest.
Arguments:
- latent: bfloat16 [16, 3072, 4096], P('queue', 'seq'), may hold values from -6 to 6
- queries: bfloat16 [16, 3072, 4096], P('queue', 'seq'), may hold values from -80.991455 to 80.991455
- key_rows: bfloat16 [16, 3072, 4096], P('queue', 'seq'), may hold values from -4 to 4
- values: bfloat16 [16, 3072, 4096], P('queue', 'seq'), may hold values from -6 to 6
- mod_table: float32 [50, 2, 4096], replicated, may hold values from -3 to 3
- levels: int32 [16], P('queue'), may hold values from 0 to 49
- fresh_noise: bfloat16 [3072, 4096], P('seq'), may hold values from -6 to 6
Outputs:
- next_latent: bfloat16 [16, 3072, 4096], P('queue', 'seq')
The draws below stay inside these ranges and needn't reach their ends.
All inputs are finite; a program needn't handle non-finite values.
Results may differ from the reference program's by a relative error of at most 0.0048.
Values may be sent and summed in bfloat16 or wider, within the bound.
No kernel may reach another device: no remote copies, remote signals or barrier semaphores. Data moves between devices by JAX's collectives and lax.ppermute only.
A program may use at most 64 MiB of HBM per device.

```python
import math
import jax
import jax.numpy as jnp
from jax import lax

HEADS = 32
HEAD_DIM = 128
STEPS = 50
HD = 4096
SEQ = 3072
GROUPS = 16


def shared_rows(key):
    return jnp.clip(jax.random.normal(key, (GROUPS, SEQ, HD), jnp.float32), -4.0, 4.0)


def draw_key_rows(key, part):
    shared = shared_rows(key)
    return shared.astype(jnp.bfloat16)


def draw_queries(key, part):
    key = jax.random.fold_in(key, 7)
    result = jnp.clip(jax.random.normal(key, (GROUPS, SEQ, HD), jnp.float32), -4.0, 4.0)
    return result.astype(jnp.bfloat16)


def plant(drawn, stream_key, smallest, high):
    longest = drawn.shape.index(max(drawn.shape))
    spots = []
    for shift in (0, 1):
        where = [jax.random.randint(jax.random.fold_in(stream_key, axis), (), 0, length) for axis, length in enumerate(drawn.shape)]
        where[longest] = (where[longest] + shift) % drawn.shape[longest]
        spots.append(tuple(where))
    return drawn.at[spots[0]].set(smallest).at[spots[1]].set(high)


def steps_of(stream_key, shape, cuts, smallest, high):
    level = 1.0
    for dim, blocks in cuts:
        heights = jax.random.uniform(jax.random.fold_in(jax.random.fold_in(stream_key, 6), dim), (blocks,), jnp.float32, smallest / len(cuts), high / len(cuts))
        level = level * jnp.repeat(jnp.exp(heights), shape[dim] // blocks).reshape((-1,) + (1,) * (len(shape) - 1 - dim))
    return level


def centred(rng, shape, scale, reach, split=(), kind=jnp.bfloat16):
    level = steps_of(rng, shape, split, -0.22, 0.18) if split else 1.0
    entries = jax.random.normal(rng, shape, jnp.float32) * scale * level
    return jnp.minimum(jnp.maximum(entries, -reach), reach).astype(kind)


def setup_inputs(seed: int = 0) -> dict:
    keys = jax.random.split(jax.random.key(seed), 8)
    latent = centred(keys[0], (GROUPS, SEQ, HD), 1.0, 6.0, ((0, 16), (1, 16)))
    queries = draw_queries(jax.random.fold_in(keys[7], 71), 0)
    key_rows = draw_key_rows(jax.random.fold_in(keys[7], 71), 0)
    values = centred(keys[3], (GROUPS, SEQ, HD), 1.0, 6.0, ((0, 16), (1, 16)))
    mod_table = centred(keys[4], (STEPS, 2, HD), 0.5, 3.0, (), jnp.float32)
    levels = plant(jax.random.randint(keys[5], (GROUPS,), 0, STEPS), jax.random.fold_in(keys[5], 1), 0, STEPS - 1).astype(jnp.int32)
    fresh_noise = centred(keys[6], (SEQ, HD), 1.0, 6.0, ((0, 16),))
    return dict(latent=latent, queries=queries, key_rows=key_rows, values=values, mod_table=mod_table, levels=levels, fresh_noise=fresh_noise)


def attend(queries, key_rows, values):
    length = queries.shape[0]
    block_rows = math.gcd(length, 512)
    block_count = length // block_rows
    factor = queries.shape[2] ** (-0.5)
    key_wide = key_rows.astype(jnp.float32)
    value_wide = values.astype(jnp.float32)
    blocks = queries.reshape(block_count, block_rows, queries.shape[1], queries.shape[2])

    def one_block(row_block):
        scores = jnp.einsum('qhd,khd->hqk', row_block.astype(jnp.float32), key_wide) * factor
        largest = lax.optimization_barrier(jnp.max(scores, axis=-1, keepdims=True))
        powers = jnp.exp(scores - largest)
        weights = (powers / lax.optimization_barrier(jnp.sum(powers, axis=-1, keepdims=True))).astype(jnp.bfloat16)
        mixed = jnp.einsum('hqk,khd->qhd', weights.astype(jnp.float32), value_wide)
        return mixed.astype(jnp.bfloat16)
    return lax.map(one_block, blocks).reshape(queries.shape)

def reference(latent, queries, key_rows, values, mod_table, levels, fresh_noise):

    def one_group(pieces):
        lat_block, query_block, key_block, value_block, level = pieces
        shape = (SEQ, HEADS, HEAD_DIM)
        attended = attend(query_block.reshape(shape), key_block.reshape(shape), value_block.reshape(shape))
        attended = attended.reshape(SEQ, HD).astype(jnp.float32)
        meansq = lax.optimization_barrier(jnp.mean(attended * attended, axis=-1, keepdims=True))
        modrow = lax.dynamic_index_in_dim(mod_table, level, 0, keepdims=False)
        velocity = (attended * lax.rsqrt(meansq + 1e-06) * (1.0 + modrow[0]) + modrow[1]).astype(jnp.bfloat16)
        velocity = lax.optimization_barrier(velocity)
        step_size = (level + 1).astype(jnp.float32) / STEPS
        return (lat_block.astype(jnp.float32) - step_size * velocity.astype(jnp.float32)).astype(jnp.bfloat16)
    denoised = lax.map(one_group, (latent, queries, key_rows, values, levels))
    return jnp.concatenate([fresh_noise[None], denoised[:-1]], axis=0)
```

```python
import functools
import math

import jax
import jax.numpy as jnp
from jax import lax
from jax.experimental import pallas as pl
from jax.experimental.pallas import tpu as pltpu
from jax.sharding import PartitionSpec as P

HEADS = 32
HEAD_DIM = 128
STEPS = 50
HALF = 8
WIDE = 256
ROWS = 192
FEATURES = HEADS * HEAD_DIM
EXPONENT = HEAD_DIM ** (-0.5) * math.log2(math.e)
GROUPS8 = [[half * HALF + k for k in range(HALF)] for half in range(2)]
NT = (((1,), (1,)), ((), ()))
PARAMS = pltpu.CompilerParams(vmem_limit_bytes=40 << 20)


def arrange(parts, half, first, rows, name):
    count = len(parts)

    def body(half_ref, *refs):
        out = refs[count]
        for i in range(count):
            out[0, :, i * WIDE : (i + 1) * WIDE] = refs[i][...]

    return pl.pallas_call(
        body,
        grid_spec=pltpu.PrefetchScalarGridSpec(
            num_scalar_prefetch=1,
            grid=(HALF,),
            in_specs=[
                pl.BlockSpec((rows, WIDE), lambda d, half_ref: (first, half_ref[0] * HALF + d))
            ]
            * count,
            out_specs=pl.BlockSpec((1, rows, count * WIDE), lambda d, half_ref: (d, 0, 0)),
        ),
        out_shape=jax.ShapeDtypeStruct((HALF, rows, count * WIDE), jnp.bfloat16),
        compiler_params=PARAMS,
        cost_estimate=pl.CostEstimate(
            flops=0, bytes_accessed=HALF * rows * count * WIDE * 4, transcendentals=0
        ),
        name=name,
    )(half, *parts)


def attend_body(chunk, q_ref, kl_ref, kr_ref, vl_ref, vr_ref, o_ref, s_ref):
    queries = q_ref[...]
    side = kl_ref.shape[0]
    largest = None
    for i, keys in enumerate((kl_ref, kr_ref)):
        for at in range(0, side, chunk):
            scores = lax.dot_general(
                queries, keys[at : at + chunk, :], NT, preferred_element_type=jnp.float32
            )
            s_ref[:, i * side + at : i * side + at + chunk] = scores
            for j in range(0, chunk, 128):
                part = scores[:, j : j + 128]
                largest = part if largest is None else jnp.maximum(largest, part)
    shift = jnp.max(largest, axis=1, keepdims=True) * EXPONENT
    total = None
    mixed = None
    for i, values in enumerate((vl_ref, vr_ref)):
        for at in range(0, side, chunk):
            powers = jnp.exp2(
                s_ref[:, i * side + at : i * side + at + chunk] * EXPONENT - shift
            )
            for j in range(0, chunk, 128):
                part = powers[:, j : j + 128]
                total = part if total is None else total + part
            product = jnp.dot(
                powers.astype(jnp.bfloat16),
                values[at : at + chunk, :],
                preferred_element_type=jnp.float32,
            )
            mixed = product if mixed is None else mixed + product
    o_ref[...] = (mixed / jnp.sum(total, axis=1, keepdims=True)).astype(jnp.bfloat16)


def attend(queries, local, remote_keys, remote_values, name):
    rows = queries.shape[0]
    side = remote_keys.shape[0]
    tile = 256
    return pl.pallas_call(
        functools.partial(attend_body, 512),
        grid=(2, rows // tile),
        in_specs=[
            pl.BlockSpec((tile, HEAD_DIM), lambda h, i: (i, h)),
            pl.BlockSpec((side, HEAD_DIM), lambda h, i: (0, h)),
            pl.BlockSpec((side, HEAD_DIM), lambda h, i: (0, h)),
            pl.BlockSpec((side, HEAD_DIM), lambda h, i: (0, 2 + h)),
            pl.BlockSpec((side, HEAD_DIM), lambda h, i: (0, h)),
        ],
        out_specs=pl.BlockSpec((tile, HEAD_DIM), lambda h, i: (i, h)),
        out_shape=jax.ShapeDtypeStruct((rows, WIDE), jnp.bfloat16),
        scratch_shapes=[pltpu.VMEM((tile, 2 * side), jnp.float32)],
        compiler_params=PARAMS,
        cost_estimate=pl.CostEstimate(
            flops=rows * 2 * side * WIDE * 4 * 3,
            bytes_accessed=6 * side * WIDE * 2,
            transcendentals=rows * 2 * side * 2,
        ),
        name=name,
    )(queries, local, remote_keys, local, remote_values)


def update_body(meta, near_ref, far_ref, latent_ref, mod_ref, fresh_ref, o_ref):
    half = meta[0]
    step_size = (meta[1] + 1).astype(jnp.float32) / STEPS
    squares = None
    for ref in (near_ref, far_ref):
        for d in range(HALF):
            part = ref[d].astype(jnp.float32)
            squares = part * part if squares is None else squares + part * part
    meansq = jnp.sum(squares, axis=1, keepdims=True) / FEATURES
    inverse = lax.rsqrt(meansq + 1e-06)
    for side, ref in enumerate((near_ref, far_ref)):
        start = (half if side == 0 else 1 - half) * (HALF * WIDE)
        for d in range(HALF):
            at = pl.ds(pl.multiple_of(start + d * WIDE, WIDE), WIDE)
            velocity = (
                ref[d].astype(jnp.float32) * inverse * (1.0 + mod_ref[0, 0:1, at])
                + mod_ref[0, 1:2, at]
            ).astype(jnp.bfloat16)
            o_ref[:, at] = (
                latent_ref[:, at].astype(jnp.float32) - step_size * velocity.astype(jnp.float32)
            ).astype(jnp.bfloat16)

    @pl.when(meta[2] == 1)
    def _():
        o_ref[...] = fresh_ref[...]


def update(meta, near, far, latent, mod_table, fresh, first, rows, name):
    tile = 48
    steps = rows // tile
    return pl.pallas_call(
        update_body,
        grid_spec=pltpu.PrefetchScalarGridSpec(
            num_scalar_prefetch=1,
            grid=(steps,),
            in_specs=[
                pl.BlockSpec((HALF, tile, WIDE), lambda i, m: (0, first * steps + i, 0)),
                pl.BlockSpec((HALF, tile, WIDE), lambda i, m: (0, i, 0)),
                pl.BlockSpec((tile, FEATURES), lambda i, m: (first * steps + i, 0)),
                pl.BlockSpec((1, 2, FEATURES), lambda i, m: (m[1], 0, 0)),
                pl.BlockSpec((tile, FEATURES), lambda i, m: (first * steps + i, 0)),
            ],
            out_specs=pl.BlockSpec((tile, FEATURES), lambda i, m: (i, 0)),
        ),
        out_shape=jax.ShapeDtypeStruct((rows, FEATURES), jnp.bfloat16),
        compiler_params=PARAMS,
        cost_estimate=pl.CostEstimate(
            flops=rows * FEATURES * 10, bytes_accessed=rows * FEATURES * 10, transcendentals=0
        ),
        name=name,
    )(meta, near, far, latent, mod_table, fresh)


def across(value):
    return lax.ppermute(value, "seq", [(s, (s + HALF) % (2 * HALF)) for s in range(2 * HALF)])


def within(value):
    return lax.all_to_all(value, "seq", 0, 0, axis_index_groups=GROUPS8)


def on_device(latent, queries, key_rows, values, mod_table, levels, fresh_noise):
    latent, queries, key_rows, values = (x[0] for x in (latent, queries, key_rows, values))
    half = lax.axis_index("seq") // HALF
    near = half.reshape(1)
    far = (1 - half).reshape(1)
    count = lax.axis_size("queue")
    group = lax.axis_index("queue")
    meta = jnp.stack([half, levels[0], (group == count - 1).astype(jnp.int32)])
    part = ROWS // 2

    far_keys = across(arrange([key_rows], far, 0, ROWS, "far_keys"))
    far_values = across(arrange([values], far, 0, ROWS, "far_values"))
    far_queries = [
        across(arrange([queries], far, i, part, f"far_queries{i}")) for i in range(2)
    ]
    local = within(arrange([key_rows, values], near, 0, ROWS, "near_keys_values"))
    local_queries = within(arrange([queries], near, 0, ROWS, "near_queries"))

    flat = lambda x: x.reshape(-1, x.shape[2])
    local = flat(local)
    far_keys = flat(within(far_keys))
    far_values = flat(within(far_values))
    mixed_near = attend(flat(local_queries), local, far_keys, far_values, "attend_near")
    mixed_near = within(mixed_near.reshape(HALF, ROWS, WIDE))
    shifted = []
    ring = [(g, (g + 1) % count) for g in range(count)]
    for i in range(2):
        rows = flat(within(far_queries[i]))
        mixed = attend(rows, local, far_keys, far_values, f"attend_far{i}")
        mixed = across(within(mixed.reshape(HALF, part, WIDE)))
        denoised = update(
            meta, mixed_near, mixed, latent, mod_table, fresh_noise, i, part, f"update{i}"
        )
        shifted.append(lax.ppermute(denoised, "queue", ring))
    return jnp.concatenate(shifted)[None]


def solution(mesh):
    return jax.shard_map(
        on_device,
        mesh=mesh,
        in_specs=(
            P("queue", "seq", None),
            P("queue", "seq", None),
            P("queue", "seq", None),
            P("queue", "seq", None),
            P(),
            P("queue"),
            P("seq", None),
        ),
        out_specs=P("queue", "seq", None),
        check_vma=False,
    )
```

```python
import functools
import math

import jax
import jax.numpy as jnp
from jax import lax
from jax.experimental import pallas as pl
from jax.experimental.pallas import tpu as pltpu
from jax.sharding import PartitionSpec as P

HEADS = 32
HEAD_DIM = 128
STEPS = 50
HALF = 8
WIDE = 256
ROWS = 192
FEATURES = HEADS * HEAD_DIM
EXPONENT = HEAD_DIM ** (-0.5) * math.log2(math.e)
GROUPS8 = [[half * HALF + k for k in range(HALF)] for half in range(2)]
NT = (((1,), (1,)), ((), ()))
SMALL = pl.CostEstimate(flops=1000, bytes_accessed=1000, transcendentals=0)
PARAMS = pltpu.CompilerParams(vmem_limit_bytes=60_000_000)


def arrange(arrays, half, layout, name):
    count = len(layout)
    width = count * WIDE

    def body(half_ref, *refs):
        sources, out, sem = refs[:count], refs[count], refs[count + 1]
        copies = [
            pltpu.make_async_copy(
                source.at[:, pl.ds(d * WIDE, WIDE)],
                out.at[d, :, pl.ds(i * WIDE, WIDE)],
                sem.at[i * HALF + d],
            )
            for i, source in enumerate(sources)
            for d in range(HALF)
        ]
        for copy in copies:
            copy.start()
        for copy in copies:
            copy.wait()

    def spec(other):
        return pl.BlockSpec((ROWS, HALF * WIDE), lambda i, h: (0, 1 - h[0] if other else h[0]))

    return pl.pallas_call(
        body,
        grid_spec=pltpu.PrefetchScalarGridSpec(
            num_scalar_prefetch=1,
            grid=(1,),
            in_specs=[spec(other) for _, other in layout],
            out_specs=pl.BlockSpec(memory_space=pl.ANY),
            scratch_shapes=[pltpu.SemaphoreType.DMA((count * HALF,))],
        ),
        out_shape=jax.ShapeDtypeStruct((HALF, ROWS, width), jnp.bfloat16),
        compiler_params=PARAMS,
        cost_estimate=SMALL,
        name=name,
    )(half, *[arrays[which] for which, _ in layout])


def attend_body(q_ref, kl_ref, kr_ref, vl_ref, vr_ref, o_ref, *s_refs):
    chunk = 512
    tile = s_refs[0].shape[0]
    queries = q_ref[...].reshape(-1, HEAD_DIM)
    side = kl_ref.shape[0]
    tiles = len(s_refs)
    states = [{} for _ in range(tiles)]
    outs = []

    def add(state, name, part, op):
        state[name] = op(state[name], part) if name in state else part

    def scores_of(t, i, at):
        keys = (kl_ref, kr_ref)[i][at : at + chunk, :]
        scores = lax.dot_general(
            queries[t * tile : (t + 1) * tile], keys, NT, preferred_element_type=jnp.float32
        )
        s_refs[t][:, i * side + at : i * side + at + chunk] = scores
        for j in range(0, chunk, 128):
            add(states[t], "largest", scores[:, j : j + 128], jnp.maximum)

    def mix(t, i, at):
        scores = s_refs[t][:, i * side + at : i * side + at + chunk]
        powers = jnp.exp2(scores * EXPONENT - states[t]["shift"])
        for j in range(0, chunk, 128):
            add(states[t], "total", powers[:, j : j + 128], jnp.add)
        product = jnp.dot(
            powers.astype(jnp.bfloat16),
            (vl_ref, vr_ref)[i][at : at + chunk, :],
            preferred_element_type=jnp.float32,
        )
        add(states[t], "mixed", product, jnp.add)

    for phase in range(tiles + 1):
        for i in range(2):
            for at in range(0, side, chunk):
                if phase < tiles:
                    scores_of(phase, i, at)
                if phase > 0:
                    mix(phase - 1, i, at)
        if phase < tiles:
            state = states[phase]
            state["shift"] = jnp.max(state["largest"], axis=1, keepdims=True) * EXPONENT
        if phase > 0:
            state = states[phase - 1]
            total = jnp.sum(state["total"], axis=1, keepdims=True)
            outs.append((state["mixed"] / total).astype(jnp.bfloat16))
    o_ref[...] = jnp.concatenate(outs).reshape(o_ref.shape)


def attend(meta, queries, near, far, rows, side_of, name, into=None, after=()):
    array, row_block, start = queries
    side = near.shape[0]
    tile = 256
    extra = ([] if into is None else [into]) + list(after)

    def body(m_ref, q_ref, kl, kr, vl, vr, *refs):
        attend_body(q_ref, kl, kr, vl, vr, *refs[len(extra) :])

    def out_index(h, m):
        return (m[0] if side_of == 0 else 1 - m[0], 0, h)

    keys = pl.BlockSpec((side, HEAD_DIM), lambda h, m: (0, h))
    values = pl.BlockSpec((side, HEAD_DIM), lambda h, m: (0, 2 + h))
    return pl.pallas_call(
        body,
        grid_spec=pltpu.PrefetchScalarGridSpec(
            num_scalar_prefetch=1,
            grid=(2,),
            in_specs=[
                pl.BlockSpec((HALF, rows, HEAD_DIM), lambda h, m: (0, row_block, start + h)),
                keys,
                keys,
                values,
                values,
            ]
            + [pl.BlockSpec(memory_space=pl.ANY)] * len(extra),
            out_specs=pl.BlockSpec((HALF, rows, HEAD_DIM), out_index),
            scratch_shapes=[pltpu.VMEM((tile, 2 * side), jnp.float32)] * (HALF * rows // tile),
        ),
        out_shape=jax.ShapeDtypeStruct((2 * HALF, rows, WIDE), jnp.bfloat16),
        input_output_aliases={} if into is None else {6: 0},
        compiler_params=PARAMS,
        cost_estimate=SMALL,
        name=name,
    )(meta, array, near, far, near, far, *extra)


def update_body(meta, mixed_ref, latent_ref, mod_ref, fresh_ref, o_ref):
    step_size = (meta[1] + 1).astype(jnp.float32) / STEPS
    squares = None
    for d in range(2 * HALF):
        part = mixed_ref[d].astype(jnp.float32)
        squares = part * part if squares is None else squares + part * part
    meansq = jnp.sum(squares, axis=1, keepdims=True) / FEATURES
    inverse = lax.rsqrt(meansq + 1e-06)
    for d in range(2 * HALF):
        at = slice(d * WIDE, (d + 1) * WIDE)
        velocity = (
            mixed_ref[d].astype(jnp.float32) * inverse * (1.0 + mod_ref[0, 0:1, at])
            + mod_ref[0, 1:2, at]
        ).astype(jnp.bfloat16)
        o_ref[:, at] = (
            latent_ref[:, at].astype(jnp.float32) - step_size * velocity.astype(jnp.float32)
        ).astype(jnp.bfloat16)

    @pl.when(meta[2] == 1)
    def _():
        o_ref[...] = fresh_ref[...]


def update(meta, mixed, latent, mod_table, fresh, first, name):
    rows = mixed.shape[1]
    tile = 48
    steps = rows // tile
    return pl.pallas_call(
        update_body,
        grid_spec=pltpu.PrefetchScalarGridSpec(
            num_scalar_prefetch=1,
            grid=(steps,),
            in_specs=[
                pl.BlockSpec((2 * HALF, tile, WIDE), lambda i, m: (0, i, 0)),
                pl.BlockSpec((tile, FEATURES), lambda i, m: (first // tile + i, 0)),
                pl.BlockSpec((1, 2, FEATURES), lambda i, m: (m[1], 0, 0)),
                pl.BlockSpec((tile, FEATURES), lambda i, m: (first // tile + i, 0)),
            ],
            out_specs=pl.BlockSpec((tile, FEATURES), lambda i, m: (i, 0)),
        ),
        out_shape=jax.ShapeDtypeStruct((rows, FEATURES), jnp.bfloat16),
        compiler_params=PARAMS,
        cost_estimate=SMALL,
        name=name,
    )(meta, mixed, latent, mod_table, fresh)


def across(value):
    return lax.ppermute(value, "seq", [(s, (s + HALF) % (2 * HALF)) for s in range(2 * HALF)])


def within(value):
    return lax.all_to_all(value, "seq", 0, 0, axis_index_groups=GROUPS8)


def on_device(latent, queries, key_rows, values, mod_table, levels, fresh_noise):
    latent, queries, key_rows, values = (x[0] for x in (latent, queries, key_rows, values))
    half = lax.axis_index("seq") // HALF
    near = half.reshape(1)
    count = lax.axis_size("queue")
    group = lax.axis_index("queue")
    meta = jnp.stack([half, levels[0], (group == count - 1).astype(jnp.int32)])
    tie = lambda x, *after: lax.optimization_barrier((x, *after))[0]
    flat = lambda x: x.reshape(-1, x.shape[2])
    always = (levels[0] | 1) != 0

    def fenced(f, *operands):
        shapes = jax.eval_shape(f, *operands)
        empty = lambda *x: jax.tree.map(lambda t: jnp.zeros(t.shape, t.dtype), shapes)
        return lax.cond(always, f, empty, *operands)

    inputs = (key_rows, values, queries)
    sent = arrange(inputs, near, [(0, True), (1, True)], "send")
    own = arrange(inputs, near, [(0, False), (1, False), (2, False)], "keep")
    out_q = arrange(inputs, near, [(2, True)], "send_q")

    far_kv = across(sent)

    def first_stage(x, y):
        x = within(x)
        return x, within(tie(y, x))

    own, far_q = fenced(first_stage, own, out_q)
    far_q = across(tie(far_q, far_kv))
    far_kv = flat(fenced(within, far_kv))
    near_kv = flat(own)
    ring = [(g, (g + 1) % count) for g in range(count)]
    chunks = ((0, 96), (96, 96))
    back = []
    last = []
    for i, (first, rows) in enumerate(chunks):
        m = attend(
            meta, (own, first // rows, 4), near_kv, far_kv, rows, 0, f"near{i}", after=last
        )
        m = attend(meta, (far_q, first // rows, 0), near_kv, far_kv, rows, 1, f"far{i}", m)
        last = [m]
        back.append(lax.all_to_all(tie(m, *back), "seq", 0, 0))
    shifted = []
    for i, (first, rows) in enumerate(chunks):
        denoised = update(meta, back[i], latent, mod_table, fresh_noise, first, f"update{i}")
        shifted.append(lax.ppermute(denoised, "queue", ring))
    return jnp.concatenate(shifted)[None]


def solution(mesh):
    return jax.shard_map(
        on_device,
        mesh=mesh,
        in_specs=(
            P("queue", "seq", None),
            P("queue", "seq", None),
            P("queue", "seq", None),
            P("queue", "seq", None),
            P(),
            P("queue"),
            P("seq", None),
        ),
        out_specs=P("queue", "seq", None),
        check_vma=False,
    )
```

```python
import functools
import math

import jax
import jax.numpy as jnp
from jax import lax
from jax.experimental import pallas as pl
from jax.experimental.pallas import tpu as pltpu
from jax.sharding import PartitionSpec as P

HEADS = 32
HEAD_DIM = 128
STEPS = 50
HALF = 8
WIDE = 256
ROWS = 192
FEATURES = HEADS * HEAD_DIM
EXPONENT = HEAD_DIM ** (-0.5) * math.log2(math.e)
GROUPS8 = [[half * HALF + k for k in range(HALF)] for half in range(2)]
NT = (((1,), (1,)), ((), ()))
SMALL = pl.CostEstimate(flops=1000, bytes_accessed=1000, transcendentals=0)
PARAMS = pltpu.CompilerParams(vmem_limit_bytes=60_000_000)


def arrange(arrays, half, layout, rows, width, name, after=()):
    count = len(layout)
    width_of = lambda head: WIDE if head is None else HEAD_DIM

    def body(half_ref, *refs):
        sources, out, sem = refs[:count], refs[-2], refs[-1]
        copies = []
        for source, (_, _, head, row, at, first, taken) in zip(sources, layout):
            w = width_of(head)
            for d in range(HALF):
                copies.append(
                    pltpu.make_async_copy(
                        source.at[
                            pl.ds(first, taken), pl.ds(d * WIDE + (head or 0) * HEAD_DIM, w)
                        ],
                        out.at[d, pl.ds(row, taken), pl.ds(at, w)],
                        sem.at[len(copies)],
                    )
                )
        for copy in copies:
            copy.start()
        for copy in copies:
            copy.wait()

    def spec(other):
        return pl.BlockSpec((ROWS, HALF * WIDE), lambda i, h: (0, 1 - h[0] if other else h[0]))

    return pl.pallas_call(
        body,
        grid_spec=pltpu.PrefetchScalarGridSpec(
            num_scalar_prefetch=1,
            grid=(1,),
            in_specs=[spec(other) for _, other, *_ in layout]
            + [pl.BlockSpec(memory_space=pl.ANY)] * len(after),
            out_specs=pl.BlockSpec(memory_space=pl.ANY),
            scratch_shapes=[pltpu.SemaphoreType.DMA((count * HALF,))],
        ),
        out_shape=jax.ShapeDtypeStruct((HALF, rows, width), jnp.bfloat16),
        compiler_params=PARAMS,
        cost_estimate=SMALL,
        name=name,
    )(half, *[arrays[which] for which, *_ in layout], *after)


def attend_body(q_ref, kl_ref, kr_ref, vl_ref, vr_ref, o_ref, *s_refs):
    chunk = 512
    tile = s_refs[0].shape[0]
    queries = q_ref[...].reshape(-1, HEAD_DIM)
    side = kl_ref.shape[0]
    tiles = len(s_refs)
    states = [{} for _ in range(tiles)]
    outs = []

    def add(state, name, part, op):
        state[name] = op(state[name], part) if name in state else part

    def scores_of(t, i, at):
        keys = (kl_ref, kr_ref)[i][at : at + chunk, :]
        scores = lax.dot_general(
            queries[t * tile : (t + 1) * tile], keys, NT, preferred_element_type=jnp.float32
        )
        s_refs[t][:, i * side + at : i * side + at + chunk] = scores
        for j in range(0, chunk, 128):
            add(states[t], "largest", scores[:, j : j + 128], jnp.maximum)

    def mix(t, i, at):
        scores = s_refs[t][:, i * side + at : i * side + at + chunk]
        powers = jnp.exp2(scores * EXPONENT - states[t]["shift"])
        for j in range(0, chunk, 128):
            add(states[t], "total", powers[:, j : j + 128], jnp.add)
        product = jnp.dot(
            powers.astype(jnp.bfloat16),
            (vl_ref, vr_ref)[i][at : at + chunk, :],
            preferred_element_type=jnp.float32,
        )
        add(states[t], "mixed", product, jnp.add)

    for phase in range(tiles + 1):
        for i in range(2):
            for at in range(0, side, chunk):
                if phase < tiles:
                    scores_of(phase, i, at)
                if phase > 0:
                    mix(phase - 1, i, at)
        if phase < tiles:
            state = states[phase]
            state["shift"] = jnp.max(state["largest"], axis=1, keepdims=True) * EXPONENT
        if phase > 0:
            state = states[phase - 1]
            total = jnp.sum(state["total"], axis=1, keepdims=True)
            outs.append((state["mixed"] / total).astype(jnp.bfloat16))
    o_ref[...] = jnp.concatenate(outs).reshape(o_ref.shape)


def attend(queries, near, far, rows, name, after=()):
    array, row_block, start = queries
    side = near.shape[0]
    tile = 256
    extra = list(after)

    def body(q_ref, kl, vl, k0, v0, k1, v1, *refs):
        o_ref, k_ref, v_ref, *s_refs = refs[len(extra) :]

        def choose(k, v):
            k_ref[...] = k[...].reshape(k_ref.shape)
            v_ref[...] = v[...].reshape(v_ref.shape)

        for h, (k, v) in enumerate(((k0, v0), (k1, v1))):
            pl.when(pl.program_id(0) == h)(functools.partial(choose, k, v))
        attend_body(q_ref, kl, k_ref, vl, v_ref, o_ref, *s_refs)

    column = lambda at: pl.BlockSpec((side, HEAD_DIM), at)
    far_columns = [
        pl.BlockSpec((HALF, ROWS, HEAD_DIM), lambda h, at=at: (0, 0, at)) for at in range(2)
    ]
    return pl.pallas_call(
        body,
        grid=(2,),
        in_specs=[
            pl.BlockSpec((HALF, rows, HEAD_DIM), lambda h: (0, row_block, start + h)),
            column(lambda h: (0, h)),
            column(lambda h: (0, 2 + h)),
        ]
        + far_columns * 2
        + [pl.BlockSpec(memory_space=pl.ANY)] * len(extra),
        out_specs=pl.BlockSpec((HALF, rows, HEAD_DIM), lambda h: (0, 0, h)),
        out_shape=jax.ShapeDtypeStruct((HALF, rows, WIDE), jnp.bfloat16),
        scratch_shapes=[pltpu.VMEM((side, HEAD_DIM), jnp.bfloat16)] * 2
        + [pltpu.VMEM((tile, 2 * side), jnp.float32)] * (HALF * rows // tile),
        compiler_params=PARAMS,
        cost_estimate=SMALL,
        name=name,
    )(array, near, near, far[0], far[0], far[1], far[1], *extra)


def update_body(half_ref, levels, mixed_ref, latent_ref, mod_ref, fresh_ref, o_ref):
    half = half_ref[0]
    step_size = (levels[0] + 1).astype(jnp.float32) / STEPS
    squares = None
    for d in range(HALF):
        for i in range(2):
            part = mixed_ref[d, :, i * WIDE : (i + 1) * WIDE].astype(jnp.float32)
            squares = part * part if squares is None else squares + part * part
    meansq = jnp.sum(squares, axis=1, keepdims=True) / FEATURES
    inverse = lax.rsqrt(meansq + 1e-06)
    for i in range(2):
        start = (half if i == 0 else 1 - half) * (HALF * WIDE)
        for d in range(HALF):
            at = pl.ds(pl.multiple_of(start + d * WIDE, WIDE), WIDE)
            velocity = (
                mixed_ref[d, :, i * WIDE : (i + 1) * WIDE].astype(jnp.float32)
                * inverse
                * (1.0 + mod_ref[0, 0:1, at])
                + mod_ref[0, 1:2, at]
            ).astype(jnp.bfloat16)
            o_ref[:, at] = (
                latent_ref[:, at].astype(jnp.float32) - step_size * velocity.astype(jnp.float32)
            ).astype(jnp.bfloat16)

    @pl.when(lax.axis_index("queue") == lax.axis_size("queue") - 1)
    def _():
        o_ref[...] = fresh_ref[...]


def update(half, levels, mixed, latent, mod_table, fresh, first, name):
    rows = mixed.shape[1]
    tile = 48
    steps = rows // tile
    plain = pl.BlockSpec((tile, FEATURES), lambda i, h, m: (first // tile + i, 0))
    return pl.pallas_call(
        update_body,
        grid_spec=pltpu.PrefetchScalarGridSpec(
            num_scalar_prefetch=2,
            grid=(steps,),
            in_specs=[
                pl.BlockSpec((HALF, tile, 2 * WIDE), lambda i, h, m: (0, i, 0)),
                plain,
                pl.BlockSpec((1, 2, FEATURES), lambda i, h, m: (m[0], 0, 0)),
                plain,
            ],
            out_specs=pl.BlockSpec((tile, FEATURES), lambda i, h, m: (i, 0)),
        ),
        out_shape=jax.ShapeDtypeStruct((rows, FEATURES), jnp.bfloat16),
        compiler_params=PARAMS,
        cost_estimate=SMALL,
        name=name,
    )(half, levels, mixed, latent, mod_table, fresh)


def across(value):
    return lax.ppermute(value, "seq", [(s, (s + HALF) % (2 * HALF)) for s in range(2 * HALF)])


def within(value):
    return lax.all_to_all(value, "seq", 0, 0, axis_index_groups=GROUPS8)


def on_device(latent, queries, key_rows, values, mod_table, levels, fresh_noise):
    latent, queries, key_rows, values = (x[0] for x in (latent, queries, key_rows, values))
    half = lax.axis_index("seq") // HALF
    near = half.reshape(1)
    count = lax.axis_size("queue")
    tie = lambda x, *after: lax.optimization_barrier((x, *after))[0] if after else x
    flat = lambda x: x.reshape(-1, x.shape[2])
    always = (levels[0] | 1) != 0

    def fenced(f, *operands):
        shapes = jax.eval_shape(f, *operands)
        empty = lambda *x: jax.tree.map(lambda t: jnp.zeros(t.shape, t.dtype), shapes)
        return lax.cond(always, f, empty, *operands)

    inputs = (key_rows, values, queries)
    chunks = ((0, 96), (96, 96))
    part = chunks[0][1]
    sent0 = arrange(
        inputs,
        near,
        [(0, True, 0, 0, 0, 0, ROWS), (1, True, 0, 0, HEAD_DIM, 0, ROWS), (2, True, None, ROWS, 0, 0, part)],
        ROWS + part,
        WIDE,
        "send0",
    )
    sent1 = arrange(
        inputs,
        near,
        [
            (0, True, 1, 0, 0, 0, ROWS),
            (1, True, 1, 0, HEAD_DIM, 0, ROWS),
            (2, True, None, ROWS, 0, part, ROWS - part),
        ],
        2 * ROWS - part,
        WIDE,
        "send1",
        [sent0],
    )
    own = arrange(
        inputs,
        near,
        [(i, False, None, 0, i * WIDE, 0, ROWS) for i in range(3)],
        ROWS,
        3 * WIDE,
        "keep",
        [sent1],
    )

    far0 = across(sent0)
    sent1 = fenced(within, sent1)
    far1 = across(sent1[:, :ROWS])
    own = fenced(within, tie(own, sent1))
    last_q = across(tie(sent1[:, ROWS:], own))
    far0 = fenced(within, tie(far0, own))
    far_q = [(far0, ROWS // part), (last_q, 0)]

    near_kv, far_kv = flat(own), (far0, far1)
    ring = [(g, (g + 1) % count) for g in range(count)]

    def far_part(i, after=()):
        array, block = far_q[i]
        return attend((tie(array, *after), block, 0), near_kv, far_kv, chunks[i][1], f"far{i}")

    def near_part(i, after):
        first, rows = chunks[i]
        return attend((tie(own, *after), first // rows, 4), near_kv, far_kv, rows, f"near{i}")

    def finish(i, back):
        first, _ = chunks[i]
        return update(near, levels, back, latent, mod_table, fresh_noise, first, f"update{i}")

    beside = lambda x, y: jnp.concatenate([x, y], axis=2)
    of_far0 = far_part(0)
    of_near0 = near_part(0, [of_far0, last_q])
    of_far1 = far_part(1, [of_near0])
    returned0, returned1 = across(of_far0), across(of_far1)

    def third_stage(x, y):
        return within(beside(x, y)), near_part(1, [])

    back0, of_near1 = fenced(third_stage, of_near0, tie(returned0, of_far1))
    denoised0 = finish(0, back0)

    def fourth_stage(x, y, z):
        return within(beside(x, y)), lax.ppermute(z, "queue", ring)

    back1, shifted0 = fenced(fourth_stage, of_near1, returned1, denoised0)
    denoised1 = finish(1, back1)
    shifted1 = lax.ppermute(denoised1, "queue", ring)
    out = tie(jnp.pad(shifted0, ((0, ROWS - shifted0.shape[0]), (0, 0))), denoised1)
    return lax.dynamic_update_slice(out, shifted1, (shifted0.shape[0], 0))[None]


def solution(mesh):
    return jax.shard_map(
        on_device,
        mesh=mesh,
        in_specs=(
            P("queue", "seq", None),
            P("queue", "seq", None),
            P("queue", "seq", None),
            P("queue", "seq", None),
            P(),
            P("queue"),
            P("seq", None),
        ),
        out_specs=P("queue", "seq", None),
        check_vma=False,
    )
```

```python
import functools
import math

import jax
import jax.numpy as jnp
from jax import lax
from jax.experimental import pallas as pl
from jax.experimental.pallas import tpu as pltpu
from jax.sharding import PartitionSpec as P

HEADS = 32
HEAD_DIM = 128
STEPS = 50
HALF = 8
WIDE = 256
ROWS = 192
FEATURES = HEADS * HEAD_DIM
EXPONENT = HEAD_DIM ** (-0.5) * math.log2(math.e)
GROUPS8 = [[half * HALF + k for k in range(HALF)] for half in range(2)]
NT = (((1,), (1,)), ((), ()))
SMALL = pl.CostEstimate(flops=1000, bytes_accessed=1000, transcendentals=0)
PARAMS = pltpu.CompilerParams(vmem_limit_bytes=60_000_000)
SLIM = pltpu.CompilerParams(vmem_limit_bytes=24 << 20)


def arrange(arrays, half, layout, rows, width, name, after=()):
    count = len(layout)
    width_of = lambda head: WIDE if head is None else HEAD_DIM

    def body(half_ref, *refs):
        sources, out, sem = refs[:count], refs[-2], refs[-1]
        copies = []
        for source, (_, _, head, row, at, first, taken) in zip(sources, layout):
            w = width_of(head)
            for d in range(HALF):
                copies.append(
                    pltpu.make_async_copy(
                        source.at[
                            pl.ds(first, taken), pl.ds(d * WIDE + (head or 0) * HEAD_DIM, w)
                        ],
                        out.at[d, pl.ds(row, taken), pl.ds(at, w)],
                        sem.at[len(copies)],
                    )
                )
        for copy in copies:
            copy.start()
        for copy in copies:
            copy.wait()

    def spec(other):
        return pl.BlockSpec((ROWS, HALF * WIDE), lambda i, h: (0, 1 - h[0] if other else h[0]))

    return pl.pallas_call(
        body,
        grid_spec=pltpu.PrefetchScalarGridSpec(
            num_scalar_prefetch=1,
            grid=(1,),
            in_specs=[spec(other) for _, other, *_ in layout]
            + [pl.BlockSpec(memory_space=pl.ANY)] * len(after),
            out_specs=pl.BlockSpec(memory_space=pl.ANY),
            scratch_shapes=[pltpu.SemaphoreType.DMA((count * HALF,))],
        ),
        out_shape=jax.ShapeDtypeStruct((HALF, rows, width), jnp.bfloat16),
        compiler_params=PARAMS,
        cost_estimate=SMALL,
        name=name,
    )(half, *[arrays[which] for which, *_ in layout], *after)


def attend_body(q_ref, keys, values, carried, o_refs, s_refs):
    chunk = 512
    tile = s_refs[0].shape[0]
    queries = q_ref[...].reshape(-1, HEAD_DIM)
    carried = [ref[...].reshape(-1, HEAD_DIM) for ref in carried]
    side = keys[0].shape[0]
    tiles = len(s_refs)
    states = [{} for _ in range(tiles)]
    outs = [[] for _ in o_refs]

    def add(state, name, part, op):
        state[name] = op(state[name], part) if name in state else part

    def scores_of(t, i, at):
        scores = lax.dot_general(
            queries[t * tile : (t + 1) * tile],
            keys[i][at : at + chunk, :],
            NT,
            preferred_element_type=jnp.float32,
        )
        s_refs[t][:, i * side + at : i * side + at + chunk] = scores
        for j in range(0, chunk, 128):
            add(states[t], "largest", scores[:, j : j + 128], jnp.maximum)

    def mix(t, i, at):
        scores = s_refs[t][:, i * side + at : i * side + at + chunk]
        powers = jnp.exp2(scores * EXPONENT - states[t]["shift"])
        for j in range(0, chunk, 128):
            add(states[t], "total", powers[:, j : j + 128], jnp.add)
        product = jnp.dot(
            powers.astype(jnp.bfloat16),
            values[i][at : at + chunk, :],
            preferred_element_type=jnp.float32,
        )
        add(states[t], "mixed", product, jnp.add)

    for phase in range(tiles + 1):
        for i in range(len(keys)):
            for at in range(0, side, chunk):
                if phase < tiles:
                    scores_of(phase, i, at)
                if phase > 0:
                    mix(phase - 1, i, at)
        if phase < tiles:
            state = states[phase]
            shift = jnp.max(state["largest"], axis=1, keepdims=True) * EXPONENT
            if carried:
                mine = slice(phase * tile, (phase + 1) * tile)
                before = carried[2][mine]
                shift = jnp.maximum(jnp.broadcast_to(shift, before.shape), before)
                rescale = jnp.exp2(before - shift)
                state["mixed"] = carried[0][mine] * rescale
                state["total"] = carried[1][mine] * rescale
                shift = shift[:, :1]
            state["shift"] = shift
        if phase > 0:
            state = states[phase - 1]
            if len(o_refs) == 3:
                shift = jnp.broadcast_to(state["shift"], (tile, HEAD_DIM))
                results = (state["mixed"], state["total"], shift)
            else:
                total = jnp.sum(state["total"], axis=1, keepdims=True)
                results = ((state["mixed"] / total).astype(jnp.bfloat16),)
            for out, result in zip(outs, results):
                out.append(result)
    for ref, out in zip(o_refs, outs):
        ref[...] = jnp.concatenate(out).reshape(ref.shape)


def attend(queries, near, far, rows, name, carried=(), partial=False):
    array, row_block, start = queries
    side = HALF * ROWS
    tile = 256
    sides = (near is not None) + (far is not None)
    column = lambda at: pl.BlockSpec((side, HEAD_DIM), at)
    operands = []
    if near is not None:
        operands += [(near, column(lambda h: (0, h))), (near, column(lambda h: (0, 2 + h)))]
    if far is not None:
        operands += [
            (x, pl.BlockSpec((HALF, ROWS, HEAD_DIM), lambda h, at=at: (0, 0, at)))
            for x in far
            for at in range(2)
        ]
    here = pl.BlockSpec((HALF, rows, HEAD_DIM), lambda h: (0, row_block, h))
    plain = pl.BlockSpec((HALF, rows, HEAD_DIM), lambda h: (0, 0, h))
    outs = 3 if partial else 1
    kind = jnp.float32 if partial else jnp.bfloat16

    def body(q_ref, *refs):
        refs = list(refs)
        take = lambda n: [refs.pop(0) for _ in range(n)]
        keys, values = [], []
        if near is not None:
            keys += take(1)
            values += take(1)
        both = take(4) if far is not None else []
        earlier = take(len(carried))
        o_refs = take(outs)
        if far is not None:
            k_ref, v_ref = take(2)

            def choose(k, v):
                k_ref[...] = k[...].reshape(k_ref.shape)
                v_ref[...] = v[...].reshape(v_ref.shape)

            for h in range(2):
                pl.when(pl.program_id(0) == h)(functools.partial(choose, *both[2 * h : 2 * h + 2]))
            keys.append(k_ref)
            values.append(v_ref)
        attend_body(q_ref, keys, values, earlier, o_refs, refs)

    result = pl.pallas_call(
        body,
        grid=(2,),
        in_specs=[pl.BlockSpec((HALF, rows, HEAD_DIM), lambda h: (0, row_block, start + h))]
        + [spec for _, spec in operands]
        + [here] * len(carried),
        out_specs=[plain] * outs,
        out_shape=[jax.ShapeDtypeStruct((HALF, rows, WIDE), kind)] * outs,
        scratch_shapes=([] if far is None else [pltpu.VMEM((side, HEAD_DIM), jnp.bfloat16)] * 2)
        + [pltpu.VMEM((tile, sides * side), jnp.float32)] * (HALF * rows // tile),
        compiler_params=SLIM,
        cost_estimate=SMALL,
        name=name,
    )(array, *[x for x, _ in operands], *carried)
    return result if partial else result[0]


def update_body(half_ref, levels, mixed_ref, latent_ref, mod_ref, fresh_ref, o_ref):
    half = half_ref[0]
    step_size = (levels[0] + 1).astype(jnp.float32) / STEPS
    squares = None
    for d in range(HALF):
        for i in range(2):
            part = mixed_ref[d, :, i * WIDE : (i + 1) * WIDE].astype(jnp.float32)
            squares = part * part if squares is None else squares + part * part
    meansq = jnp.sum(squares, axis=1, keepdims=True) / FEATURES
    inverse = lax.rsqrt(meansq + 1e-06)
    for i in range(2):
        start = (half if i == 0 else 1 - half) * (HALF * WIDE)
        for d in range(HALF):
            at = pl.ds(pl.multiple_of(start + d * WIDE, WIDE), WIDE)
            velocity = (
                mixed_ref[d, :, i * WIDE : (i + 1) * WIDE].astype(jnp.float32)
                * inverse
                * (1.0 + mod_ref[0, 0:1, at])
                + mod_ref[0, 1:2, at]
            ).astype(jnp.bfloat16)
            o_ref[:, at] = (
                latent_ref[:, at].astype(jnp.float32) - step_size * velocity.astype(jnp.float32)
            ).astype(jnp.bfloat16)

    @pl.when(lax.axis_index("queue") == lax.axis_size("queue") - 1)
    def _():
        o_ref[...] = fresh_ref[...]


def update(half, levels, mixed, latent, mod_table, fresh, first, name):
    rows = mixed.shape[1]
    tile = 48
    steps = rows // tile
    plain = pl.BlockSpec((tile, FEATURES), lambda i, h, m: (first // tile + i, 0))
    return pl.pallas_call(
        update_body,
        grid_spec=pltpu.PrefetchScalarGridSpec(
            num_scalar_prefetch=2,
            grid=(steps,),
            in_specs=[
                pl.BlockSpec((HALF, tile, 2 * WIDE), lambda i, h, m: (0, i, 0)),
                plain,
                pl.BlockSpec((1, 2, FEATURES), lambda i, h, m: (m[0], 0, 0)),
                plain,
            ],
            out_specs=pl.BlockSpec((tile, FEATURES), lambda i, h, m: (i, 0)),
        ),
        out_shape=jax.ShapeDtypeStruct((rows, FEATURES), jnp.bfloat16),
        compiler_params=SLIM,
        cost_estimate=SMALL,
        name=name,
    )(half, levels, mixed, latent, mod_table, fresh)


def across(value):
    return lax.ppermute(value, "seq", [(s, (s + HALF) % (2 * HALF)) for s in range(2 * HALF)])


def within(value):
    return lax.all_to_all(value, "seq", 0, 0, axis_index_groups=GROUPS8)


def on_device(latent, queries, key_rows, values, mod_table, levels, fresh_noise):
    latent, queries, key_rows, values = (x[0] for x in (latent, queries, key_rows, values))
    half = lax.axis_index("seq") // HALF
    near = half.reshape(1)
    count = lax.axis_size("queue")
    tie = lambda x, *after: lax.optimization_barrier((x, *after))[0] if after else x
    flat = lambda x: x.reshape(-1, x.shape[2])
    always = (levels[0] | 1) != 0

    def fenced(f, *operands):
        shapes = jax.eval_shape(f, *operands)
        empty = lambda *x: jax.tree.map(lambda t: jnp.zeros(t.shape, t.dtype), shapes)
        return lax.cond(always, f, empty, *operands)

    inputs = (key_rows, values, queries)
    chunks = ((0, 96), (96, 96))
    part = chunks[0][1]
    sent0 = arrange(
        inputs,
        near,
        [(0, True, 0, 0, 0, 0, ROWS), (1, True, 0, 0, HEAD_DIM, 0, ROWS), (2, True, None, ROWS, 0, 0, part)],
        ROWS + part,
        WIDE,
        "send0",
    )
    sent1 = arrange(
        inputs,
        near,
        [
            (0, True, 1, 0, 0, 0, ROWS),
            (1, True, 1, 0, HEAD_DIM, 0, ROWS),
            (2, True, None, ROWS, 0, part, ROWS - part),
        ],
        2 * ROWS - part,
        WIDE,
        "send1",
        [sent0],
    )
    own = arrange(
        inputs,
        near,
        [(i, False, None, 0, i * WIDE, 0, ROWS) for i in range(3)],
        ROWS,
        3 * WIDE,
        "keep",
        [sent1],
    )

    far0 = across(sent0)
    sent1 = fenced(within, sent1)
    far1 = across(sent1[:, :ROWS])
    own = fenced(within, tie(own, sent1))
    last_q = across(tie(sent1[:, ROWS:], own))
    def second_stage(x, y):
        return within(x), attend((y, 0, 4), flat(y), None, ROWS, "near", partial=True)

    far0, early = fenced(second_stage, tie(far0, own), own)
    far_q = [(far0, ROWS // part), (last_q, 0)]

    near_kv, far_kv = flat(own), (far0, far1)
    ring = [(g, (g + 1) % count) for g in range(count)]

    def far_part(i, after=()):
        array, block = far_q[i]
        return attend((tie(array, *after), block, 0), near_kv, far_kv, chunks[i][1], f"far{i}")

    def near_part(i, after):
        first, rows = chunks[i]
        queries = (tie(own, *after), first // rows, 4)
        return attend(queries, None, far_kv, rows, f"near{i}", early)

    def finish(i, back):
        first, _ = chunks[i]
        return update(near, levels, back, latent, mod_table, fresh_noise, first, f"update{i}")

    beside = lambda x, y: jnp.concatenate([x, y], axis=2)
    of_far0 = far_part(0)
    of_near0 = near_part(0, [of_far0, last_q])
    of_far1 = far_part(1, [of_near0])
    returned0, returned1 = across(of_far0), across(of_far1)

    def third_stage(x, y):
        return within(beside(x, y)), near_part(1, [])

    back0, of_near1 = fenced(third_stage, of_near0, tie(returned0, of_far1))
    denoised0 = finish(0, back0)

    def fourth_stage(x, y, z):
        return finish(1, within(beside(x, y))), lax.ppermute(z, "queue", ring)

    denoised1, shifted0 = fenced(fourth_stage, of_near1, returned1, denoised0)
    shifted1 = lax.ppermute(denoised1, "queue", ring)
    out = tie(jnp.pad(shifted0, ((0, ROWS - shifted0.shape[0]), (0, 0))), denoised1)
    return lax.dynamic_update_slice(out, shifted1, (shifted0.shape[0], 0))[None]


def solution(mesh):
    return jax.shard_map(
        on_device,
        mesh=mesh,
        in_specs=(
            P("queue", "seq", None),
            P("queue", "seq", None),
            P("queue", "seq", None),
            P("queue", "seq", None),
            P(),
            P("queue"),
            P("seq", None),
        ),
        out_specs=P("queue", "seq", None),
        check_vma=False,
    )
```

```python
import functools
import math

import jax
import jax.numpy as jnp
from jax import lax
from jax.experimental import pallas as pl
from jax.experimental.pallas import tpu as pltpu
from jax.sharding import PartitionSpec as P

HEADS = 32
HEAD_DIM = 128
STEPS = 50
HALF = 8
WIDE = 256
ROWS = 192
FEATURES = HEADS * HEAD_DIM
EXPONENT = HEAD_DIM ** (-0.5) * math.log2(math.e)
GROUPS8 = [[half * HALF + k for k in range(HALF)] for half in range(2)]
NT = (((1,), (1,)), ((), ()))
SMALL = pl.CostEstimate(flops=1000, bytes_accessed=1000, transcendentals=0)
PARAMS = pltpu.CompilerParams(vmem_limit_bytes=60_000_000)
SLIM = pltpu.CompilerParams(vmem_limit_bytes=24 << 20)


def arrange(arrays, half, layout, rows, width, name, after=()):
    count = len(layout)
    width_of = lambda head: WIDE if head is None else HEAD_DIM

    def body(half_ref, *refs):
        sources, out, sem = refs[:count], refs[-2], refs[-1]
        copies = []
        for source, (_, _, head, row, at, first, taken) in zip(sources, layout):
            w = width_of(head)
            for d in range(HALF):
                copies.append(
                    pltpu.make_async_copy(
                        source.at[
                            pl.ds(first, taken), pl.ds(d * WIDE + (head or 0) * HEAD_DIM, w)
                        ],
                        out.at[d, pl.ds(row, taken), pl.ds(at, w)],
                        sem.at[len(copies)],
                    )
                )
        for copy in copies:
            copy.start()
        for copy in copies:
            copy.wait()

    def spec(other):
        return pl.BlockSpec((ROWS, HALF * WIDE), lambda i, h: (0, 1 - h[0] if other else h[0]))

    return pl.pallas_call(
        body,
        grid_spec=pltpu.PrefetchScalarGridSpec(
            num_scalar_prefetch=1,
            grid=(1,),
            in_specs=[spec(other) for _, other, *_ in layout]
            + [pl.BlockSpec(memory_space=pl.ANY)] * len(after),
            out_specs=pl.BlockSpec(memory_space=pl.ANY),
            scratch_shapes=[pltpu.SemaphoreType.DMA((count * HALF,))],
        ),
        out_shape=jax.ShapeDtypeStruct((HALF, rows, width), jnp.bfloat16),
        compiler_params=PARAMS,
        cost_estimate=SMALL,
        name=name,
    )(half, *[arrays[which] for which, *_ in layout], *after)


def attend_body(q_ref, keys, values, carried, o_refs, s_refs):
    chunk = 512
    tile = s_refs[0].shape[0]
    queries = q_ref[...].reshape(-1, HEAD_DIM)
    carried = [ref[...].reshape(-1, HEAD_DIM) for ref in carried]
    side = keys[0].shape[0]
    tiles = len(s_refs)
    states = [{} for _ in range(tiles)]
    outs = [[] for _ in o_refs]

    def add(state, name, part, op):
        state[name] = op(state[name], part) if name in state else part

    def scores_of(t, i, at):
        scores = lax.dot_general(
            queries[t * tile : (t + 1) * tile],
            keys[i][at : at + chunk, :],
            NT,
            preferred_element_type=jnp.float32,
        )
        s_refs[t][:, i * side + at : i * side + at + chunk] = scores
        for j in range(0, chunk, 128):
            add(states[t], "largest", scores[:, j : j + 128], jnp.maximum)

    def mix(t, i, at):
        scores = s_refs[t][:, i * side + at : i * side + at + chunk]
        powers = jnp.exp2(scores * EXPONENT - states[t]["shift"])
        for j in range(0, chunk, 128):
            add(states[t], "total", powers[:, j : j + 128], jnp.add)
        product = jnp.dot(
            powers.astype(jnp.bfloat16),
            values[i][at : at + chunk, :],
            preferred_element_type=jnp.float32,
        )
        add(states[t], "mixed", product, jnp.add)

    for phase in range(tiles + 1):
        for i in range(len(keys)):
            for at in range(0, side, chunk):
                if phase < tiles:
                    scores_of(phase, i, at)
                if phase > 0:
                    mix(phase - 1, i, at)
        if phase < tiles:
            state = states[phase]
            shift = jnp.max(state["largest"], axis=1, keepdims=True) * EXPONENT
            if carried:
                mine = slice(phase * tile, (phase + 1) * tile)
                before = carried[2][mine]
                shift = jnp.maximum(jnp.broadcast_to(shift, before.shape), before)
                rescale = jnp.exp2(before - shift)
                state["mixed"] = carried[0][mine] * rescale
                state["total"] = carried[1][mine] * rescale
                shift = shift[:, :1]
            state["shift"] = shift
        if phase > 0:
            state = states[phase - 1]
            if len(o_refs) == 3:
                shift = jnp.broadcast_to(state["shift"], (tile, HEAD_DIM))
                results = (state["mixed"], state["total"], shift)
            else:
                total = jnp.sum(state["total"], axis=1, keepdims=True)
                results = ((state["mixed"] / total).astype(jnp.bfloat16),)
            for out, result in zip(outs, results):
                out.append(result)
    for ref, out in zip(o_refs, outs):
        ref[...] = jnp.concatenate(out).reshape(ref.shape)


def attend(queries, near, far, rows, name, carried=(), partial=False):
    array, row_block, start = queries
    side = HALF * ROWS
    tile = 256
    sides = (near is not None) + (far is not None)
    column = lambda at: pl.BlockSpec((side, HEAD_DIM), at)
    operands = []
    if near is not None:
        operands += [(near, column(lambda h: (0, h))), (near, column(lambda h: (0, 2 + h)))]
    if far is not None:
        operands += [
            (x, pl.BlockSpec((HALF, ROWS, HEAD_DIM), lambda h, at=at: (0, 0, at)))
            for x in far
            for at in range(2)
        ]
    here = pl.BlockSpec((HALF, rows, HEAD_DIM), lambda h: (0, row_block, h))
    plain = pl.BlockSpec((HALF, rows, HEAD_DIM), lambda h: (0, 0, h))
    outs = 3 if partial else 1
    kind = jnp.float32 if partial else jnp.bfloat16

    def body(q_ref, *refs):
        refs = list(refs)
        take = lambda n: [refs.pop(0) for _ in range(n)]
        keys, values = [], []
        if near is not None:
            keys += take(1)
            values += take(1)
        both = take(4) if far is not None else []
        earlier = take(len(carried))
        o_refs = take(outs)
        if far is not None:
            k_ref, v_ref = take(2)

            def choose(k, v):
                k_ref[...] = k[...].reshape(k_ref.shape)
                v_ref[...] = v[...].reshape(v_ref.shape)

            for h in range(2):
                pl.when(pl.program_id(0) == h)(functools.partial(choose, *both[2 * h : 2 * h + 2]))
            keys.append(k_ref)
            values.append(v_ref)
        attend_body(q_ref, keys, values, earlier, o_refs, refs)

    result = pl.pallas_call(
        body,
        grid=(2,),
        in_specs=[pl.BlockSpec((HALF, rows, HEAD_DIM), lambda h: (0, row_block, start + h))]
        + [spec for _, spec in operands]
        + [here] * len(carried),
        out_specs=[plain] * outs,
        out_shape=[jax.ShapeDtypeStruct((HALF, rows, WIDE), kind)] * outs,
        scratch_shapes=([] if far is None else [pltpu.VMEM((side, HEAD_DIM), jnp.bfloat16)] * 2)
        + [pltpu.VMEM((tile, sides * side), jnp.float32)] * (HALF * rows // tile),
        compiler_params=SLIM,
        cost_estimate=SMALL,
        name=name,
    )(array, *[x for x, _ in operands], *carried)
    return result if partial else result[0]


def update_body(first, half_ref, levels, mixed_ref, latent_ref, mod_ref, fresh_ref, o_ref):
    half = half_ref[0]
    step_size = (levels[0] + 1).astype(jnp.float32) / STEPS
    squares = None
    for d in range(HALF):
        for i in range(2):
            part = mixed_ref[d, :, i * WIDE : (i + 1) * WIDE].astype(jnp.float32)
            squares = part * part if squares is None else squares + part * part
    meansq = jnp.sum(squares, axis=1, keepdims=True) / FEATURES
    inverse = lax.rsqrt(meansq + 1e-06)
    for i in range(2):
        start = (half if i == 0 else 1 - half) * (HALF * WIDE)
        for d in range(HALF):
            at = pl.ds(pl.multiple_of(start + d * WIDE, WIDE), WIDE)
            velocity = (
                mixed_ref[d, :, i * WIDE : (i + 1) * WIDE].astype(jnp.float32)
                * inverse
                * (1.0 + mod_ref[0, 0:1, at])
                + mod_ref[0, 1:2, at]
            ).astype(jnp.bfloat16)
            o_ref[:, at] = (
                latent_ref[:, at].astype(jnp.float32) - step_size * velocity.astype(jnp.float32)
            ).astype(jnp.bfloat16)

    @pl.when(lax.axis_index("queue") == lax.axis_size("queue") - 1)
    def _():
        rows = o_ref.shape[0]
        start = pl.multiple_of(first + pl.program_id(0) * rows, 16)
        pltpu.sync_copy(fresh_ref.at[pl.ds(start, rows)], o_ref)


def update(half, levels, mixed, latent, mod_table, fresh, first, name):
    rows = mixed.shape[1]
    tile = 48
    steps = rows // tile
    plain = pl.BlockSpec((tile, FEATURES), lambda i, h, m: (first // tile + i, 0))
    return pl.pallas_call(
        functools.partial(update_body, first),
        grid_spec=pltpu.PrefetchScalarGridSpec(
            num_scalar_prefetch=2,
            grid=(steps,),
            in_specs=[
                pl.BlockSpec((HALF, tile, 2 * WIDE), lambda i, h, m: (0, i, 0)),
                plain,
                pl.BlockSpec((1, 2, FEATURES), lambda i, h, m: (m[0], 0, 0)),
                pl.BlockSpec(memory_space=pl.ANY),
            ],
            out_specs=pl.BlockSpec((tile, FEATURES), lambda i, h, m: (i, 0)),
        ),
        out_shape=jax.ShapeDtypeStruct((rows, FEATURES), jnp.bfloat16),
        compiler_params=SLIM,
        cost_estimate=SMALL,
        name=name,
    )(half, levels, mixed, latent, mod_table, fresh)


def across(value):
    return lax.ppermute(value, "seq", [(s, (s + HALF) % (2 * HALF)) for s in range(2 * HALF)])


def within(value):
    return lax.all_to_all(value, "seq", 0, 0, axis_index_groups=GROUPS8)


def on_device(latent, queries, key_rows, values, mod_table, levels, fresh_noise):
    latent, queries, key_rows, values = (x[0] for x in (latent, queries, key_rows, values))
    half = lax.axis_index("seq") // HALF
    near = half.reshape(1)
    count = lax.axis_size("queue")
    tie = lambda x, *after: lax.optimization_barrier((x, *after))[0] if after else x
    flat = lambda x: x.reshape(-1, x.shape[2])
    always = (levels[0] | 1) != 0

    def fenced(f, *operands):
        shapes = jax.eval_shape(f, *operands)
        empty = lambda *x: jax.tree.map(lambda t: jnp.zeros(t.shape, t.dtype), shapes)
        return lax.cond(always, f, empty, *operands)

    inputs = (key_rows, values, queries)
    chunks = ((0, 96), (96, 96))
    part = chunks[0][1]
    sent0 = arrange(
        inputs,
        near,
        [(0, True, 0, 0, 0, 0, ROWS), (1, True, 0, 0, HEAD_DIM, 0, ROWS), (2, True, None, ROWS, 0, 0, part)],
        ROWS + part,
        WIDE,
        "send0",
    )
    sent1 = arrange(
        inputs,
        near,
        [
            (0, True, 1, 0, 0, 0, ROWS),
            (1, True, 1, 0, HEAD_DIM, 0, ROWS),
            (2, True, None, ROWS, 0, part, ROWS - part),
        ],
        2 * ROWS - part,
        WIDE,
        "send1",
        [sent0],
    )
    own = arrange(
        inputs,
        near,
        [(i, False, None, 0, i * WIDE, 0, ROWS) for i in range(3)],
        ROWS,
        3 * WIDE,
        "keep",
        [sent1],
    )

    far0 = across(sent0)
    sent1 = fenced(within, sent1)
    far1 = across(sent1[:, :ROWS])
    own = fenced(within, tie(own, sent1))
    last_q = across(tie(sent1[:, ROWS:], own))
    def second_stage(x, y):
        return within(x), attend((y, 0, 4), flat(y), None, ROWS, "near", partial=True)

    far0, early = fenced(second_stage, tie(far0, own), own)
    far_q = [(far0, ROWS // part), (last_q, 0)]

    near_kv, far_kv = flat(own), (far0, far1)
    ring = [(g, (g + 1) % count) for g in range(count)]

    def far_part(i, after=()):
        array, block = far_q[i]
        return attend((tie(array, *after), block, 0), near_kv, far_kv, chunks[i][1], f"far{i}")

    def near_part(i, after):
        first, rows = chunks[i]
        queries = (tie(own, *after), first // rows, 4)
        return attend(queries, None, far_kv, rows, f"near{i}", early)

    def finish(i, back):
        first, _ = chunks[i]
        return update(near, levels, back, latent, mod_table, fresh_noise, first, f"update{i}")

    beside = lambda x, y: jnp.concatenate([x, y], axis=2)
    of_far0 = far_part(0)
    of_near0 = near_part(0, [of_far0, last_q])
    of_far1 = far_part(1, [of_near0])
    returned0, returned1 = across(of_far0), across(of_far1)

    def third_stage(x, y):
        return within(beside(x, y)), near_part(1, [])

    back0, of_near1 = fenced(third_stage, of_near0, tie(returned0, of_far1))
    denoised0 = finish(0, back0)

    def fourth_stage(x, y, z):
        return finish(1, within(beside(x, y))), lax.ppermute(z, "queue", ring)

    denoised1, shifted0 = fenced(fourth_stage, of_near1, returned1, denoised0)
    shifted1 = lax.ppermute(denoised1, "queue", ring)
    out = tie(jnp.pad(shifted0, ((0, ROWS - shifted0.shape[0]), (0, 0))), denoised1)
    return lax.dynamic_update_slice(out, shifted1, (shifted0.shape[0], 0))[None]


def solution(mesh):
    return jax.shard_map(
        on_device,
        mesh=mesh,
        in_specs=(
            P("queue", "seq", None),
            P("queue", "seq", None),
            P("queue", "seq", None),
            P("queue", "seq", None),
            P(),
            P("queue"),
            P("seq", None),
        ),
        out_specs=P("queue", "seq", None),
        check_vma=False,
    )
```
